256 devices in a mesh: section: 16 (over y, z_lo, core), seq: 16 (over x, z_hi).
Axes of the slice: x: 4, y: 4, z: 8 (z_hi: 4, z_lo: 2; z = z_hi * 2 + z_lo), core: 2. Of those that a mesh axis runs over, the one named last changes fastest.
Arguments:
- stream: bfloat16 [16, 2048, 4096], P('section', 'seq'), may hold values from -6 to 6
- depth_weights: float32 [16, 4], P('section'), may hold values from 0.3 to 1
- depth_reach: int32 [16], P('section'), may hold values from 0 to 3, as said below
- norm_gain: float32 [16, 4096], P('section'), may hold values from 0.1 to 1.9
- qkv_weight: bfloat16 [16, 4096, 32, 3, 128], P('section', None, 'seq'), may hold values from -3 to 3
Outputs:
- layer_input: bfloat16 [16, 2048, 4096], P('section', 'seq')
- attended: bfloat16 [16, 2048, 4096], P('section', 'seq')
The draws below stay inside these ranges and needn't reach their ends.
Inputs may be any that keep to these rules, and one draw needn't show every extreme that they name: depth_reach[s] is 0 or min(3, s // 4); the last layer carries a depth average and layer 14 does not.
All inputs are finite; a program needn't handle non-finite values.
Results may differ from the reference program's by a relative error of at most 0.0083.
Values may be sent and summed in bfloat16 or wider, within the bound.
A program may use at most 128 MiB of HBM per device.

```python
import jax
import jax.numpy as jnp
from jax import lax

D = 4096
HEADS = 32
HD = 128
TOKENS = 2048
SECTIONS = 16
SPACING = 4


def draw_depth_reach(key, part):
    key = jax.random.fold_in(key, 5)
    carries = jax.random.randint(key, (SECTIONS,), 0, 2, jnp.int32)
    places = jnp.arange(SECTIONS, dtype=jnp.int32)
    carries = jnp.where(places == SECTIONS - 1, 1, carries)
    carries = jnp.where(places == SECTIONS - 2, 0, carries)
    return carries * jnp.minimum(places // SPACING, 3)


def draw_qkv_weight(key, part):
    key = jax.random.fold_in(key, 7)
    first_key, second_key, third_key = jax.random.split(key, 3)
    shape = (SECTIONS, D, HEADS, HD)
    spread = D ** (-0.5)
    key_part = jax.random.truncated_normal(first_key, -4.0, 4.0, shape, jnp.float32) * spread
    value_part = jax.random.truncated_normal(second_key, -4.0, 4.0, shape, jnp.float32) * spread
    other_part = jax.random.truncated_normal(third_key, -4.0, 4.0, shape, jnp.float32) * spread
    query_part = other_part
    return jnp.stack([query_part, key_part, value_part], axis=3).astype(jnp.bfloat16)


def shard_levels(key, shape, cuts, low, high):
    gain = 1.0
    for dim, shards_of in cuts:
        draws = jax.random.uniform(jax.random.fold_in(jax.random.fold_in(key, 6), dim), (shards_of,), jnp.float32, low / len(cuts), high / len(cuts))
        gain = gain * jnp.repeat(jnp.exp(draws), shape[dim] // shards_of).reshape((-1,) + (1,) * (len(shape) - 1 - dim))
    return gain


def normal_values(rng, dims, scale, bound, cuts=(), kind=jnp.bfloat16):
    result = jax.random.normal(rng, dims, jnp.float32) * scale
    if len(cuts) > 0:
        result = shard_levels(rng, dims, cuts, -0.22, 0.18) * result
    return jnp.clip(result, min=-bound, max=bound).astype(kind)


def setup_inputs(seed: int = 0) -> dict:
    seeds = jax.random.split(jax.random.key(seed), 6)
    stream = normal_values(seeds[0], (SECTIONS, TOKENS, D), 1.0, 6.0, ((0, 16), (1, 16)))
    depth_weights = jnp.clip(0.3 + 0.7 * jax.random.uniform(seeds[1], (SECTIONS, 4), jnp.float32) ** shard_levels(seeds[1], (SECTIONS, 4), ((0, 16),), -0.2, 0.2), 0.3, 1.0)
    depth_reach = draw_depth_reach(jax.random.fold_in(seeds[5], 71), 0)
    norm_gain = jnp.clip(1.0 + 0.18 * jax.random.normal(seeds[3], (SECTIONS, D), jnp.float32), 0.1, 1.9)
    qkv_weight = draw_qkv_weight(jax.random.fold_in(seeds[5], 71), 0)
    return {"stream": stream, "depth_weights": depth_weights, "depth_reach": depth_reach, "norm_gain": norm_gain, "qkv_weight": qkv_weight}


def attend_heads(projected):
    total_rows = projected.shape[0]
    block = min(512, total_rows)
    factor = projected.shape[-1] ** (-0.5)
    outputs = []
    for begin_row in range(0, total_rows, block):
        end_row = begin_row + block
        query_rows = projected[begin_row:end_row, :, 0, :]
        key_rows = projected[:end_row, :, 1, :]
        value_rows = projected[:end_row, :, 2, :]
        scores = jnp.einsum('qhe,khe->hqk', query_rows, key_rows, preferred_element_type=jnp.float32) * factor
        row_place = begin_row + lax.broadcasted_iota(jnp.int32, (block, end_row), 0)
        col_place = lax.broadcasted_iota(jnp.int32, (block, end_row), 1)
        scores = jnp.where(col_place <= row_place, scores, -jnp.inf)
        row_max = lax.optimization_barrier(jnp.max(scores, axis=-1, keepdims=True))
        raw_weights = jnp.exp(scores - row_max)
        attention = (raw_weights / lax.optimization_barrier(jnp.sum(raw_weights, axis=-1, keepdims=True))).astype(jnp.bfloat16)
        outputs.append(jnp.einsum('hqk,khe->qhe', attention, value_rows, preferred_element_type=jnp.float32).astype(jnp.bfloat16))
    return jnp.concatenate(outputs, axis=0)

def reference(stream, depth_weights, depth_reach, norm_gain, qkv_weight):

    def one_section(position):
        coefficients = depth_weights[position]
        reach_here = depth_reach[position]
        depth_mix = coefficients[0] * stream[position].astype(jnp.float32)
        for distance in range(1, 4):
            source = position - distance * SPACING
            earlier = stream[jnp.maximum(source, 0)].astype(jnp.float32)
            present = (source >= 0) & (distance <= reach_here)
            weight_now = jnp.where(present, coefficients[distance], jnp.zeros((), coefficients.dtype))
            depth_mix = depth_mix + weight_now * earlier
        layer_input = depth_mix.astype(jnp.bfloat16)
        mean_square = lax.optimization_barrier(jnp.mean(depth_mix * depth_mix, axis=-1, keepdims=True))
        normed = (depth_mix * lax.rsqrt(mean_square + 1e-05) * norm_gain[position]).astype(jnp.bfloat16)
        projected = jnp.einsum('rd,dhce->rhce', normed, qkv_weight[position], preferred_element_type=jnp.float32).astype(jnp.bfloat16)
        attended = attend_heads(projected)
        return (layer_input, attended.reshape(TOKENS, HEADS * HD))
    layer_input, attended = lax.map(one_section, jnp.arange(SECTIONS, dtype=jnp.int32))
    return (layer_input, attended)
```

```python
import jax
import jax.numpy as jnp
from jax import lax
from jax.experimental import pallas as pl
from jax.experimental.pallas import tpu as pltpu
from jax.sharding import PartitionSpec as P

MESH = pl.DeviceIdType.MESH
SIDE = 4
PEERS = SIDE * SIDE
CHUNKS = 8
ROWS = 16
SPACING = 4
REACH = 3
D = 4096
HD = 128
SPLIT = 3200


def wrap(value):
    return lax.rem(value + 2 * SIDE, SIDE)


def kernel(
    weights_ref, reach_ref, stream_ref, gain_ref, w_hbm,
    layer_ref, out_ref,
    gathered, earlier, w_ref, mix, qkv, attended,
    send_sem, recv_sem, depth_send, depth_recv, w_sem, out_send, out_recv, own_sem,
):
    section = lax.axis_index("section")
    me = lax.axis_index("seq")
    layer_y = section // SPACING
    x, z = me // SIDE, lax.rem(me, SIDE)

    w_copy = pltpu.make_async_copy(w_hbm, w_ref, w_sem)
    w_copy.start()

    barrier = pltpu.get_barrier_semaphore()
    for step in range(1, PEERS):
        pl.semaphore_signal(
            barrier, inc=1,
            device_id={"seq": lax.rem(me + step, PEERS)}, device_id_type=MESH,
        )
    for step in range(1, SIDE):
        pl.semaphore_signal(
            barrier, inc=1,
            device_id={"section": lax.rem(section + step * SPACING, SIDE * SPACING)},
            device_id_type=MESH,
        )
    pl.semaphore_wait(barrier, PEERS - 1 + SIDE - 1)

    def depth_copy(chunk, distance):
        return pltpu.make_async_remote_copy(
            src_ref=stream_ref.at[chunk],
            dst_ref=earlier.at[distance - 1, chunk],
            send_sem=depth_send.at[distance - 1, chunk],
            recv_sem=depth_recv.at[distance - 1, chunk],
            device_id={"section": lax.rem(section + distance * SPACING, SIDE * SPACING)},
            device_id_type=MESH,
        )

    def start_depth(chunk):
        for distance in range(1, REACH + 1):
            @pl.when(layer_y + distance < SIDE)
            def _():
                depth_copy(chunk, distance).start()

    def columns(part):
        return pl.ds(0, SPLIT) if part == 0 else pl.ds(SPLIT, D - SPLIT)

    def place(part, major, minor):
        return minor * SIDE + major if part == 0 else major * SIDE + minor

    def block_copy(part, chunk, origin, target):
        block = gathered.at[chunk, origin, :, columns(part)]
        return pltpu.make_async_remote_copy(
            src_ref=block,
            dst_ref=block,
            send_sem=send_sem.at[part, chunk],
            recv_sem=recv_sem.at[part, chunk, origin],
            device_id={"seq": target},
            device_id_type=MESH,
        )

    def arrive(part, chunk, origin):
        block_copy(part, chunk, origin, lax.rem(me + 1, PEERS)).wait_recv()

    spots = ((z, x), (x, z))

    def own(chunk):
        for distance in range(1, REACH + 1):
            @pl.when(layer_y >= distance)
            def _():
                depth_copy(chunk, distance).wait_recv()
        mix[...] = weights_ref[0, 0] * stream_ref[chunk].astype(jnp.float32)
        for distance in range(1, REACH + 1):
            @pl.when(layer_y >= distance)
            def _():
                now = jnp.where(distance <= reach_ref[0], weights_ref[0, distance], 0.0)
                mix[...] += now * earlier[distance - 1, chunk].astype(jnp.float32)
        value = mix[...]
        layer_ref[chunk] = value.astype(jnp.bfloat16)
        square = jnp.mean(value * value, axis=-1, keepdims=True)
        gathered[chunk, me] = (value * lax.rsqrt(square + 1e-05) * gain_ref[...]).astype(
            jnp.bfloat16
        )
        for part in (0, 1):
            major, minor = spots[part]
            for by in (1, -1):
                block_copy(part, chunk, me, place(part, wrap(major + by), minor)).start()
            for by in (1, -1):
                block_copy(part, chunk, me, place(part, major, wrap(minor + by))).start()

    def turn_of(chunk):
        return 1 - 2 * lax.rem(chunk, 2)

    def spread(chunk):
        turn = turn_of(chunk)
        for index, by in enumerate((-1, 1, 2)):
            for part in (0, 1):
                major, minor = spots[part]
                origin = place(part, wrap(major + by * turn), minor)
                arrive(part, chunk, origin)
                if index == 0:
                    block_copy(part, chunk, origin, place(part, wrap(major + turn), minor)).start()
                for side in (1, -1):
                    block_copy(
                        part, chunk, origin, place(part, major, wrap(minor + side))
                    ).start()

    rows_of = ((0, 1), (-1, -1), (1, -1), (2, 1))

    def relay(chunk):
        turn = turn_of(chunk)
        for by, way in rows_of:
            for part in (0, 1):
                major, minor = spots[part]
                row = wrap(major + by * turn)
                origin = place(part, row, wrap(minor - way * turn))
                arrive(part, chunk, origin)
                block_copy(
                    part, chunk, origin, place(part, major, wrap(minor + way * turn))
                ).start()

    def finish(chunk):
        turn = turn_of(chunk)
        for by, way in rows_of:
            for part in (0, 1):
                major, minor = spots[part]
                row = wrap(major + by * turn)
                arrive(part, chunk, place(part, row, wrap(minor + way * turn)))
                arrive(part, chunk, place(part, row, wrap(minor + 2)))
        block = gathered[chunk].reshape(PEERS * ROWS, D)
        for tile in range(3):
            product = jnp.dot(
                block, w_ref[:, tile * 256:(tile + 1) * 256],
                preferred_element_type=jnp.float32,
            ).astype(jnp.bfloat16)
            for half in range(2):
                qkv[2 * tile + half, :, chunk] = product[
                    :, half * HD:(half + 1) * HD
                ].reshape(PEERS, ROWS, HD)

    for chunk in range(2):
        start_depth(chunk)

    @pl.loop(0, CHUNKS + 3)
    def _(step):
        @pl.when(step < CHUNKS)
        def _():
            own(step)

        @pl.when(step + 2 < CHUNKS)
        def _():
            start_depth(step + 2)

        @pl.when((step >= 1) & (step < CHUNKS + 1))
        def _():
            spread(step - 1)

        @pl.when((step >= 2) & (step < CHUNKS + 2))
        def _():
            relay(step - 2)

        @pl.when(step == 3)
        def _():
            w_copy.wait()

        @pl.when(step >= 3)
        def _():
            finish(step - 3)

    scale = (HD ** -0.5) * 1.4426950408889634
    across = (((1,), (1,)), ((), ()))

    def attend(block):
        size = 2 * CHUNKS * ROWS
        row = lax.broadcasted_iota(jnp.int32, (size, size), 0)
        column = lax.broadcasted_iota(jnp.int32, (size, size), 1)
        for head in range(2):
            query = qkv[3 * head, 2 * block:2 * block + 2].reshape(size, HD)
            pieces = [(2 * block, 2 * block + 2)]
            if block > 0:
                pieces.append((0, 2 * block))
            scores = []
            for begin, end in pieces:
                key = qkv[3 * head + 1, begin:end].reshape((end - begin) * HD, HD)
                scores.append(
                    lax.dot_general(query, key, across, preferred_element_type=jnp.float32)
                )
            scores[0] = jnp.where(column <= row, scores[0], -jnp.inf)
            top = jnp.max(scores[0], axis=-1, keepdims=True)
            if block > 0:
                top = jnp.maximum(top, jnp.max(scores[1], axis=-1, keepdims=True))
            total, result = 0.0, 0.0
            for (begin, end), score in zip(pieces, scores):
                raw = jnp.exp2((score - top) * scale)
                total = total + jnp.sum(raw, axis=-1, keepdims=True)
                value = qkv[3 * head + 2, begin:end].reshape((end - begin) * HD, HD)
                result = result + jnp.dot(
                    raw.astype(jnp.bfloat16), value, preferred_element_type=jnp.float32
                )
            attended[2 * block:2 * block + 2, :, head * HD:(head + 1) * HD] = (
                (result / total).astype(jnp.bfloat16).reshape(2, HD, HD)
            )

    lanes = out_ref.at[:, pl.ds(pl.multiple_of(me * 2 * HD, 2 * HD), 2 * HD)]
    keep = pltpu.make_async_copy(attended.at[me], lanes, own_sem)

    @pl.loop(0, PEERS // 2)
    def _(step):
        block = lax.rem(me // 2 + 1 + step, PEERS // 2)
        for variant in range(PEERS // 2):
            @pl.when(block == variant)
            def _():
                attend(variant)
        for half in range(2):
            target = 2 * block + half

            @pl.when(target != me)
            def _():
                pltpu.make_async_remote_copy(
                    src_ref=attended.at[target],
                    dst_ref=lanes,
                    send_sem=out_send,
                    recv_sem=out_recv,
                    device_id={"seq": target},
                    device_id_type=MESH,
                ).start()

    keep.start()
    for part in (0, 1):
        @pl.loop(0, CHUNKS)
        def _(chunk):
            sent = gathered.at[chunk, pl.ds(0, PEERS - 1), :, columns(part)]
            pltpu.make_async_copy(sent, sent, send_sem.at[part, chunk]).wait()
    for distance in range(1, REACH + 1):
        @pl.when(layer_y + distance < SIDE)
        def _():
            @pl.loop(0, CHUNKS)
            def _(chunk):
                depth_copy(chunk, distance).wait_send()
    keep.wait()
    moved = attended.at[pl.ds(0, PEERS - 1)]
    pltpu.make_async_copy(moved, moved, out_send).wait()
    pltpu.make_async_copy(moved, moved, out_recv).wait()


def local(stream, depth_weights, depth_reach, norm_gain, qkv_weight):
    vmem = pl.BlockSpec(memory_space=pltpu.VMEM)
    smem = pl.BlockSpec(memory_space=pltpu.SMEM)
    layer, attended = pl.pallas_call(
        kernel,
        out_shape=(
            jax.ShapeDtypeStruct((CHUNKS, ROWS, D), jnp.bfloat16),
            jax.ShapeDtypeStruct((CHUNKS * ROWS, D), jnp.bfloat16),
        ),
        in_specs=[smem, smem, vmem, vmem, pl.BlockSpec(memory_space=pl.ANY)],
        out_specs=(vmem, vmem),
        scratch_shapes=[
            pltpu.VMEM((CHUNKS, PEERS, ROWS, D), jnp.bfloat16),
            pltpu.VMEM((REACH, CHUNKS, ROWS, D), jnp.bfloat16),
            pltpu.VMEM((D, 6 * HD), jnp.bfloat16),
            pltpu.VMEM((ROWS, D), jnp.float32),
            pltpu.VMEM((6, PEERS, CHUNKS, ROWS, HD), jnp.bfloat16),
            pltpu.VMEM((PEERS, HD, 2 * HD), jnp.bfloat16),
            pltpu.SemaphoreType.DMA((2, CHUNKS)),
            pltpu.SemaphoreType.DMA((2, CHUNKS, PEERS)),
            pltpu.SemaphoreType.DMA((REACH, CHUNKS)),
            pltpu.SemaphoreType.DMA((REACH, CHUNKS)),
            pltpu.SemaphoreType.DMA,
            pltpu.SemaphoreType.DMA,
            pltpu.SemaphoreType.DMA,
            pltpu.SemaphoreType.DMA,
        ],
        compiler_params=pltpu.CompilerParams(
            collective_id=0, has_side_effects=True, vmem_limit_bytes=56 * 1024 * 1024
        ),
        cost_estimate=pl.CostEstimate(
            flops=16_000_000_000, bytes_accessed=12_000_000, transcendentals=5_000_000
        ),
    )(
        depth_weights, depth_reach,
        stream.reshape(CHUNKS, ROWS, D), norm_gain, qkv_weight.reshape(D, 6 * HD),
    )
    return layer.reshape(stream.shape), attended[None]


def solution(mesh):
    placed = (
        P("section", "seq", None),
        P("section", None),
        P("section"),
        P("section", None),
        P("section", None, "seq", None, None),
    )
    return jax.shard_map(
        local,
        mesh=mesh,
        in_specs=placed,
        out_specs=(P("section", "seq", None), P("section", "seq", None)),
        check_vma=False,
    )
```

```python
import jax
import jax.numpy as jnp
from jax import lax
from jax.experimental import pallas as pl
from jax.experimental.pallas import tpu as pltpu
from jax.sharding import PartitionSpec as P

MESH = pl.DeviceIdType.MESH
SIDE = 4
PEERS = SIDE * SIDE
CHUNKS = 8
ROWS = 16
SPACING = 4
REACH = 3
D = 4096
HD = 128
W_ROWS = 256
PIECES = 4
HEAD_START = 2
PARTS = 1
UNITS = CHUNKS * PARTS
WIDTH = D // PARTS
SPLIT = 3328


def wrap(value):
    return lax.rem(value + 2 * SIDE, SIDE)


def kernel(
    weights_ref, reach_ref, stream_ref, gain_ref, w_hbm,
    layer_ref, out_ref,
    gathered, earlier, w_raw, w_wide, w_ref, layer, mix, qkv, attended,
    send_sem, recv_sem, depth_send, depth_recv, w_sem, out_send, out_recv, own_sem, layer_sem, turn_sem,
):
    section = lax.axis_index("section")
    me = lax.axis_index("seq")
    layer_y = section // SPACING
    x, z = me // SIDE, lax.rem(me, SIDE)

    w_copy = pltpu.make_async_copy(w_hbm, w_raw, w_sem)
    w_copy.start()

    barrier = pltpu.get_barrier_semaphore()
    for step in range(1, PEERS):
        pl.semaphore_signal(
            barrier, inc=1,
            device_id={"seq": lax.rem(me + step, PEERS)}, device_id_type=MESH,
        )
    for step in range(1, SIDE):
        pl.semaphore_signal(
            barrier, inc=1,
            device_id={"section": lax.rem(section + step * SPACING, SIDE * SPACING)},
            device_id_type=MESH,
        )
    mate = section + 1 - 2 * lax.rem(section, 2)
    pl.semaphore_signal(barrier, inc=1, device_id={"section": mate}, device_id_type=MESH)
    pl.semaphore_wait(barrier, PEERS - 1 + SIDE - 1 + 1)
    leads = lax.rem(section, 2) == 0

    def depth_copy(chunk, distance):
        return pltpu.make_async_remote_copy(
            src_ref=stream_ref.at[chunk],
            dst_ref=earlier.at[distance - 1, chunk],
            send_sem=depth_send.at[distance - 1, chunk],
            recv_sem=depth_recv.at[distance - 1, chunk],
            device_id={"section": lax.rem(section + distance * SPACING, SIDE * SPACING)},
            device_id_type=MESH,
        )

    def start_depth(chunk):
        for distance in range(1, REACH + 1):
            @pl.when(layer_y + distance < SIDE)
            def _():
                depth_copy(chunk, distance).start()

    def layer_copy(chunk):
        return pltpu.make_async_copy(layer.at[chunk], layer_ref.at[chunk], layer_sem.at[chunk])

    def columns(part, unit, fold=None):
        begin = lax.rem(unit, PARTS) * WIDTH + (0 if part == 0 else SPLIT)
        size = SPLIT if part == 0 else WIDTH - SPLIT
        if fold is not None:
            near = size // 256 * 128
            begin, size = (begin, near) if fold == 0 else (begin + near, size - near)
        return pl.ds(pl.multiple_of(begin, 128), size)

    def place(part, major, minor):
        return minor * SIDE + major if part == 0 else major * SIDE + minor

    def block_copy(part, unit, origin, target, fold=None):
        block = gathered.at[unit // PARTS, origin, :, columns(part, unit, fold)]
        return pltpu.make_async_remote_copy(
            src_ref=block,
            dst_ref=block,
            send_sem=send_sem.at[part, unit],
            recv_sem=recv_sem.at[part, unit, PEERS if fold == 1 else origin],
            device_id={"seq": target},
            device_id_type=MESH,
        )

    def arrive(part, unit, origin, fold=None):
        block_copy(part, unit, origin, lax.rem(me + 1, PEERS), fold).wait_recv()

    spots = ((z, x), (x, z))

    def mix_rows(chunk):
        for distance in range(1, REACH + 1):
            @pl.when(layer_y >= distance)
            def _():
                depth_copy(chunk, distance).wait_recv()
        mix[...] = weights_ref[0, 0] * stream_ref[chunk].astype(jnp.float32)
        for distance in range(1, REACH + 1):
            @pl.when(layer_y >= distance)
            def _():
                now = jnp.where(distance <= reach_ref[0], weights_ref[0, distance], 0.0)
                mix[...] += now * earlier[distance - 1, chunk].astype(jnp.float32)
        value = mix[...]
        layer[chunk] = value.astype(jnp.bfloat16)
        layer_copy(chunk).start()
        square = jnp.mean(value * value, axis=-1, keepdims=True)
        gathered[chunk, me] = (value * lax.rsqrt(square + 1e-05) * gain_ref[...]).astype(
            jnp.bfloat16
        )
    def own(unit):
        @pl.when(lax.rem(unit, PARTS) == 0)
        def _():
            mix_rows(unit // PARTS)

        for part in (0, 1):
            major, minor = spots[part]
            for by in (1, -1):
                block_copy(part, unit, me, place(part, wrap(major + by), minor)).start()
            for by in (1, -1):
                block_copy(part, unit, me, place(part, major, wrap(minor + by))).start()

    def aside(part, unit, origin):
        major, minor = spots[part]
        for side in (1, -1):
            block_copy(part, unit, origin, place(part, major, wrap(minor + side))).start()

    def spread_near(unit):
        for part in (0, 1):
            major, minor = spots[part]
            for fold, by in enumerate((-1, 1)):
                origin = place(part, wrap(major + by), minor)
                arrive(part, unit, origin)
                block_copy(part, unit, origin, place(part, wrap(major - by), minor), fold).start()
                aside(part, unit, origin)

    def spread_far(unit):
        for part in (0, 1):
            major, minor = spots[part]
            origin = place(part, wrap(major + 2), minor)
            for fold in (0, 1):
                arrive(part, unit, origin, fold)
            aside(part, unit, origin)

    rows_of = ((0, 1), (-1, -1), (1, -1), (2, 1))

    def relay(unit, rows):
        for by, way in rows:
            for part in (0, 1):
                major, minor = spots[part]
                origin = place(part, wrap(major + by), wrap(minor - way))
                arrive(part, unit, origin)
                block_copy(part, unit, origin, place(part, major, wrap(minor + way))).start()

    def finish(unit):
        for by, way in rows_of:
            for part in (0, 1):
                major, minor = spots[part]
                row = wrap(major + by)
                arrive(part, unit, place(part, row, wrap(minor + way)))
                arrive(part, unit, place(part, row, wrap(minor + 2)))

        @pl.when(lax.rem(unit, PARTS) == PARTS - 1)
        def _():
            project(unit // PARTS)

    def project(chunk):
        block = gathered[chunk].reshape(PEERS * ROWS, D)
        for tile in range(3):
            product = jnp.dot(
                block, w_ref[:, tile * 256:(tile + 1) * 256],
                preferred_element_type=jnp.float32,
            ).astype(jnp.bfloat16)
            for half in range(2):
                qkv[2 * tile + half, :, chunk] = product[
                    :, half * HD:(half + 1) * HD
                ].reshape(PEERS, ROWS, HD)

    @pl.when(jnp.logical_not(leads))
    def _():
        pl.semaphore_wait(turn_sem, 1)

    start_depth(0)

    w_copy.wait()

    @pl.loop(0, D // W_ROWS)
    def _(part):
        begin = pl.multiple_of(part * W_ROWS, W_ROWS)
        w_wide[...] = w_raw[pl.ds(pl.multiple_of(part * W_ROWS * 6, W_ROWS * 6), W_ROWS * 6)].astype(
            jnp.float32
        )
        for piece in range(6):
            w_ref[pl.ds(begin, W_ROWS), piece * HD:(piece + 1) * HD] = w_wide[
                pl.ds(piece, W_ROWS, stride=6)
            ].astype(jnp.bfloat16)

    start_depth(1)

    @pl.loop(0, UNITS + 4)
    def _(step):
        def when(lag, work):
            @pl.when((step >= lag) & (step < UNITS + lag))
            def _():
                work(step - lag)

        when(0, own)

        @pl.when((lax.rem(step, PARTS) == 0) & (step // PARTS + 2 < CHUNKS))
        def _():
            start_depth(step // PARTS + 2)

        when(1, spread_near)
        when(2, lambda unit: relay(unit, rows_of[:3]))

        @pl.when(leads & (step == HEAD_START))
        def _():
            pl.semaphore_signal(turn_sem, inc=1, device_id={"section": mate}, device_id_type=MESH)

        when(2, spread_far)
        when(3, lambda unit: relay(unit, rows_of[3:]))
        when(4, finish)

    scale = (HD ** -0.5) * 1.4426950408889634
    across = (((1,), (1,)), ((), ()))

    def attend(block):
        size = 2 * CHUNKS * ROWS
        row = lax.broadcasted_iota(jnp.int32, (size, size), 0)
        column = lax.broadcasted_iota(jnp.int32, (size, size), 1)
        for head in range(2):
            query = qkv[head, 2 * block:2 * block + 2].reshape(size, HD)
            pieces = [(2 * block, 2 * block + 2)]
            if block > 0:
                pieces.append((0, 2 * block))
            scores = []
            for begin, end in pieces:
                key = qkv[2 + head, begin:end].reshape((end - begin) * HD, HD)
                scores.append(
                    lax.dot_general(query, key, across, preferred_element_type=jnp.float32)
                )
            scores[0] = jnp.where(column <= row, scores[0], -jnp.inf)
            top = jnp.max(scores[0], axis=-1, keepdims=True)
            if block > 0:
                top = jnp.maximum(top, jnp.max(scores[1], axis=-1, keepdims=True))
            total, result = 0.0, 0.0
            for (begin, end), score in zip(pieces, scores):
                raw = jnp.exp2((score - top) * scale)
                total = total + jnp.sum(raw, axis=-1, keepdims=True)
                value = qkv[4 + head, begin:end].reshape((end - begin) * HD, HD)
                result = result + jnp.dot(
                    raw.astype(jnp.bfloat16), value, preferred_element_type=jnp.float32
                )
            attended[2 * block:2 * block + 2, :, head * HD:(head + 1) * HD] = (
                (result / total).astype(jnp.bfloat16).reshape(2, HD, HD)
            )

    lanes = out_ref.at[:, pl.ds(pl.multiple_of(me * 2 * HD, 2 * HD), 2 * HD)]
    keep = pltpu.make_async_copy(attended.at[me], lanes, own_sem)

    @pl.loop(0, PEERS // 2)
    def _(step):
        block = lax.rem(me // 2 + 1 + step, PEERS // 2)
        for variant in range(PEERS // 2):
            @pl.when(block == variant)
            def _():
                attend(variant)
        for half in range(2):
            target = 2 * block + half

            @pl.when(target != me)
            def _():
                pltpu.make_async_remote_copy(
                    src_ref=attended.at[target],
                    dst_ref=lanes,
                    send_sem=out_send,
                    recv_sem=out_recv,
                    device_id={"seq": target},
                    device_id_type=MESH,
                ).start()

    keep.start()
    for part in (0, 1):
        @pl.loop(0, UNITS)
        def _(unit):
            sent = gathered.at[unit // PARTS, pl.ds(0, PEERS - 1), :, columns(part, unit)]
            pltpu.make_async_copy(sent, sent, send_sem.at[part, unit]).wait()
    for distance in range(1, REACH + 1):
        @pl.when(layer_y + distance < SIDE)
        def _():
            @pl.loop(0, CHUNKS)
            def _(chunk):
                depth_copy(chunk, distance).wait_send()
    @pl.loop(0, CHUNKS)
    def _(chunk):
        layer_copy(chunk).wait()

    keep.wait()
    moved = attended.at[pl.ds(0, PEERS - 1)]
    pltpu.make_async_copy(moved, moved, out_send).wait()
    pltpu.make_async_copy(moved, moved, out_recv).wait()


def hand_over(layer, attended, layer_out, attended_out):
    layer_out[...] = layer[...]
    attended_out[...] = attended[...]


def local(stream, depth_weights, depth_reach, norm_gain, qkv_weight):
    vmem = pl.BlockSpec(memory_space=pltpu.VMEM)
    smem = pl.BlockSpec(memory_space=pltpu.SMEM)
    layer, attended = pl.pallas_call(
        kernel,
        out_shape=(
            jax.ShapeDtypeStruct((CHUNKS, ROWS, D), jnp.bfloat16),
            jax.ShapeDtypeStruct((CHUNKS * ROWS, D), jnp.bfloat16),
        ),
        in_specs=[smem, smem, vmem, vmem, pl.BlockSpec(memory_space=pl.ANY)],
        out_specs=(pl.BlockSpec(memory_space=pl.ANY),) * 2,
        scratch_shapes=[
            pltpu.VMEM((CHUNKS, PEERS, ROWS, D), jnp.bfloat16),
            pltpu.VMEM((REACH, CHUNKS, ROWS, D), jnp.bfloat16),
            pltpu.VMEM((D * 6, HD), jnp.bfloat16),
            pltpu.VMEM((W_ROWS * 6, HD), jnp.float32),
            pltpu.VMEM((D, 6 * HD), jnp.bfloat16),
            pltpu.VMEM((CHUNKS, ROWS, D), jnp.bfloat16),
            pltpu.VMEM((ROWS, D), jnp.float32),
            pltpu.VMEM((6, PEERS, CHUNKS, ROWS, HD), jnp.bfloat16),
            pltpu.VMEM((PEERS, HD, 2 * HD), jnp.bfloat16),
            pltpu.SemaphoreType.DMA((2, UNITS)),
            pltpu.SemaphoreType.DMA((2, UNITS, PEERS + 1)),
            pltpu.SemaphoreType.DMA((REACH, CHUNKS)),
            pltpu.SemaphoreType.DMA((REACH, CHUNKS)),
            pltpu.SemaphoreType.DMA,
            pltpu.SemaphoreType.DMA,
            pltpu.SemaphoreType.DMA,
            pltpu.SemaphoreType.DMA,
            pltpu.SemaphoreType.DMA((CHUNKS,)),
            pltpu.SemaphoreType.REGULAR,
        ],
        compiler_params=pltpu.CompilerParams(
            collective_id=0, has_side_effects=True, vmem_limit_bytes=56 * 1024 * 1024
        ),
        cost_estimate=pl.CostEstimate(
            flops=16_000_000_000, bytes_accessed=12_000_000, transcendentals=5_000_000
        ),
    )(
        depth_weights, depth_reach,
        stream.reshape(CHUNKS, ROWS, D), norm_gain, jnp.transpose(qkv_weight[0], (0, 2, 1, 3)).reshape(D * 6, HD),
    )
    layer, attended = pl.pallas_call(
        hand_over,
        out_shape=(jax.ShapeDtypeStruct((CHUNKS * ROWS, D), jnp.bfloat16),) * 2,
        grid=(PIECES,),
        in_specs=[pl.BlockSpec((CHUNKS * ROWS // PIECES, D), lambda i: (i, 0))] * 2,
        out_specs=(pl.BlockSpec((CHUNKS * ROWS // PIECES, D), lambda i: (i, 0)),) * 2,
    )(layer.reshape(CHUNKS * ROWS, D), attended)
    return layer[None], attended[None]


def solution(mesh):
    placed = (
        P("section", "seq", None),
        P("section", None),
        P("section"),
        P("section", None),
        P("section", None, "seq", None, None),
    )
    return jax.shard_map(
        local,
        mesh=mesh,
        in_specs=placed,
        out_specs=(P("section", "seq", None), P("section", "seq", None)),
        check_vma=False,
    )
```

```python
import jax
import jax.numpy as jnp
from jax import lax
from jax.experimental import pallas as pl
from jax.experimental.pallas import tpu as pltpu
from jax.sharding import PartitionSpec as P

MESH = pl.DeviceIdType.MESH
SIDE = 4
PEERS = SIDE * SIDE
CHUNKS = 8
ROWS = 16
SPACING = 4
REACH = 3
D = 4096
HD = 128
W_ROWS = 256
LAGS = (2, 4, 6, 8)
HEAD_START = 6
PARTS = 2
UNITS = CHUNKS * PARTS
WIDTH = D // PARTS
SPLIT = 1664


def wrap(value):
    return lax.rem(value + 2 * SIDE, SIDE)


def kernel(
    weights_ref, reach_ref, stream_hbm, gain_ref, w_hbm,
    layer_ref, out_ref,
    stream_ref, gathered, earlier, w_raw, w_wide, w_ref, mix, qkv, attended,
    send_sem, recv_sem, depth_send, depth_recv, w_sem, out_send, out_recv, own_sem, stream_sem, turn_sem,
):
    section = lax.axis_index("section")
    me = lax.axis_index("seq")
    layer_y = section // SPACING
    x, z = me // SIDE, lax.rem(me, SIDE)

    barrier = pltpu.get_barrier_semaphore()
    for step in range(1, PEERS):
        pl.semaphore_signal(
            barrier, inc=1,
            device_id={"seq": lax.rem(me + step, PEERS)}, device_id_type=MESH,
        )
    for step in range(1, SIDE):
        pl.semaphore_signal(
            barrier, inc=1,
            device_id={"section": lax.rem(section + step * SPACING, SIDE * SPACING)},
            device_id_type=MESH,
        )
    mate = section + 1 - 2 * lax.rem(section, 2)
    pl.semaphore_signal(barrier, inc=1, device_id={"section": mate}, device_id_type=MESH)
    stream_copy = pltpu.make_async_copy(stream_hbm, stream_ref, stream_sem)
    stream_copy.start()
    w_copy = pltpu.make_async_copy(w_hbm, w_raw, w_sem)
    w_copy.start()
    pl.semaphore_wait(barrier, PEERS - 1 + SIDE - 1 + 1)
    leads = lax.rem(section, 2) == 0

    def depth_copy(chunk, distance):
        return pltpu.make_async_remote_copy(
            src_ref=stream_ref.at[chunk],
            dst_ref=earlier.at[distance - 1, chunk],
            send_sem=depth_send.at[distance - 1, chunk],
            recv_sem=depth_recv.at[distance - 1, chunk],
            device_id={"section": lax.rem(section + distance * SPACING, SIDE * SPACING)},
            device_id_type=MESH,
        )

    def start_depth(chunk):
        for distance in range(1, REACH + 1):
            @pl.when(layer_y + distance < SIDE)
            def _():
                depth_copy(chunk, distance).start()

    def columns(part, unit, fold=None):
        begin = lax.rem(unit, PARTS) * WIDTH + (0 if part == 0 else SPLIT)
        size = SPLIT if part == 0 else WIDTH - SPLIT
        if fold is not None:
            near = size // 256 * 128
            begin, size = (begin, near) if fold == 0 else (begin + near, size - near)
        return pl.ds(pl.multiple_of(begin, 128), size)

    def place(part, major, minor):
        return minor * SIDE + major if part == 0 else major * SIDE + minor

    def block_copy(part, unit, origin, target, fold=None):
        block = gathered.at[unit // PARTS, origin, :, columns(part, unit, fold)]
        return pltpu.make_async_remote_copy(
            src_ref=block,
            dst_ref=block,
            send_sem=send_sem.at[part, unit],
            recv_sem=recv_sem.at[part, unit, PEERS if fold == 1 else origin],
            device_id={"seq": target},
            device_id_type=MESH,
        )

    def arrive(part, unit, origin, fold=None):
        block_copy(part, unit, origin, lax.rem(me + 1, PEERS), fold).wait_recv()

    spots = ((z, x), (x, z))

    def mix_rows(chunk):
        for distance in range(1, REACH + 1):
            @pl.when(layer_y >= distance)
            def _():
                depth_copy(chunk, distance).wait_recv()
        mix[...] = weights_ref[0, 0] * stream_ref[chunk].astype(jnp.float32)
        for distance in range(1, REACH + 1):
            @pl.when(layer_y >= distance)
            def _():
                now = jnp.where(distance <= reach_ref[0], weights_ref[0, distance], 0.0)
                mix[...] += now * earlier[distance - 1, chunk].astype(jnp.float32)
        value = mix[...]
        layer_ref[chunk] = value.astype(jnp.bfloat16)
        square = jnp.mean(value * value, axis=-1, keepdims=True)
        gathered[chunk, me] = (value * lax.rsqrt(square + 1e-05) * gain_ref[...]).astype(
            jnp.bfloat16
        )
    def own(unit):
        @pl.when(lax.rem(unit, PARTS) == 0)
        def _():
            mix_rows(unit // PARTS)

        for part in (0, 1):
            major, minor = spots[part]
            for by in (1, -1):
                block_copy(part, unit, me, place(part, wrap(major + by), minor)).start()
            for by in (1, -1):
                block_copy(part, unit, me, place(part, major, wrap(minor + by))).start()

    def aside(part, unit, origin):
        major, minor = spots[part]
        for side in (1, -1):
            block_copy(part, unit, origin, place(part, major, wrap(minor + side))).start()

    def spread_near(unit):
        for part in (0, 1):
            major, minor = spots[part]
            for fold, by in enumerate((-1, 1)):
                origin = place(part, wrap(major + by), minor)
                arrive(part, unit, origin)
                block_copy(part, unit, origin, place(part, wrap(major - by), minor), fold).start()
                aside(part, unit, origin)

    def spread_far(unit):
        for part in (0, 1):
            major, minor = spots[part]
            origin = place(part, wrap(major + 2), minor)
            for fold in (0, 1):
                arrive(part, unit, origin, fold)
            aside(part, unit, origin)

    rows_of = ((0, 1), (-1, -1), (1, -1), (2, 1))

    def relay(unit, rows):
        for by, way in rows:
            for part in (0, 1):
                major, minor = spots[part]
                origin = place(part, wrap(major + by), wrap(minor - way))
                arrive(part, unit, origin)
                block_copy(part, unit, origin, place(part, major, wrap(minor + way))).start()

    def finish(unit):
        for by, way in rows_of:
            for part in (0, 1):
                major, minor = spots[part]
                row = wrap(major + by)
                arrive(part, unit, place(part, row, wrap(minor + way)))
                arrive(part, unit, place(part, row, wrap(minor + 2)))

        @pl.when(lax.rem(unit, PARTS) == PARTS - 1)
        def _():
            project(unit // PARTS)

    def project(chunk):
        block = gathered[chunk].reshape(PEERS * ROWS, D)
        for tile in range(3):
            product = jnp.dot(
                block, w_ref[:, tile * 256:(tile + 1) * 256],
                preferred_element_type=jnp.float32,
            ).astype(jnp.bfloat16)
            for half in range(2):
                qkv[2 * tile + half, :, chunk] = product[
                    :, half * HD:(half + 1) * HD
                ].reshape(PEERS, ROWS, HD)

    stream_copy.wait()

    @pl.when(jnp.logical_not(leads))
    def _():
        pl.semaphore_wait(turn_sem, 1)

    start_depth(0)

    w_copy.wait()

    @pl.loop(0, D // W_ROWS)
    def _(part):
        begin = pl.multiple_of(part * W_ROWS, W_ROWS)
        w_wide[...] = w_raw[pl.ds(pl.multiple_of(part * W_ROWS * 6, W_ROWS * 6), W_ROWS * 6)].astype(
            jnp.float32
        )
        for piece in range(6):
            w_ref[pl.ds(begin, W_ROWS), piece * HD:(piece + 1) * HD] = w_wide[
                pl.ds(piece, W_ROWS, stride=6)
            ].astype(jnp.bfloat16)

    start_depth(1)

    @pl.loop(0, UNITS + LAGS[3])
    def _(step):
        def when(lag, work):
            @pl.when((step >= lag) & (step < UNITS + lag))
            def _():
                work(step - lag)

        when(0, own)

        @pl.when((lax.rem(step, PARTS) == 0) & (step // PARTS + 2 < CHUNKS))
        def _():
            start_depth(step // PARTS + 2)

        when(LAGS[0], spread_near)
        when(LAGS[1], lambda unit: relay(unit, rows_of[:3]))

        @pl.when(leads & (step == HEAD_START))
        def _():
            pl.semaphore_signal(turn_sem, inc=1, device_id={"section": mate}, device_id_type=MESH)

        when(LAGS[1], spread_far)
        when(LAGS[2], lambda unit: relay(unit, rows_of[3:]))
        when(LAGS[3], finish)

    scale = (HD ** -0.5) * 1.4426950408889634
    across = (((1,), (1,)), ((), ()))

    def attend(block):
        size = 2 * CHUNKS * ROWS
        row = lax.broadcasted_iota(jnp.int32, (size, size), 0)
        column = lax.broadcasted_iota(jnp.int32, (size, size), 1)
        for head in range(2):
            query = qkv[head, 2 * block:2 * block + 2].reshape(size, HD)
            pieces = [(2 * block, 2 * block + 2)]
            if block > 0:
                pieces.append((0, 2 * block))
            scores = []
            for begin, end in pieces:
                key = qkv[2 + head, begin:end].reshape((end - begin) * HD, HD)
                scores.append(
                    lax.dot_general(query, key, across, preferred_element_type=jnp.float32)
                )
            scores[0] = jnp.where(column <= row, scores[0], -jnp.inf)
            top = jnp.max(scores[0], axis=-1, keepdims=True)
            if block > 0:
                top = jnp.maximum(top, jnp.max(scores[1], axis=-1, keepdims=True))
            total, result = 0.0, 0.0
            for (begin, end), score in zip(pieces, scores):
                raw = jnp.exp2((score - top) * scale)
                total = total + jnp.sum(raw, axis=-1, keepdims=True)
                value = qkv[4 + head, begin:end].reshape((end - begin) * HD, HD)
                result = result + jnp.dot(
                    raw.astype(jnp.bfloat16), value, preferred_element_type=jnp.float32
                )
            attended[2 * block:2 * block + 2, :, head * HD:(head + 1) * HD] = (
                (result / total).astype(jnp.bfloat16).reshape(2, HD, HD)
            )

    lanes = out_ref.at[:, pl.ds(pl.multiple_of(me * 2 * HD, 2 * HD), 2 * HD)]
    keep = pltpu.make_async_copy(attended.at[me], lanes, own_sem)

    @pl.loop(0, PEERS // 2)
    def _(step):
        block = lax.rem(me // 2 + 1 + step, PEERS // 2)
        for variant in range(PEERS // 2):
            @pl.when(block == variant)
            def _():
                attend(variant)
        for half in range(2):
            target = 2 * block + half

            @pl.when(target != me)
            def _():
                pltpu.make_async_remote_copy(
                    src_ref=attended.at[target],
                    dst_ref=lanes,
                    send_sem=out_send,
                    recv_sem=out_recv,
                    device_id={"seq": target},
                    device_id_type=MESH,
                ).start()

    keep.start()
    for part in (0, 1):
        @pl.loop(0, UNITS)
        def _(unit):
            sent = gathered.at[unit // PARTS, pl.ds(0, PEERS - 1), :, columns(part, unit)]
            pltpu.make_async_copy(sent, sent, send_sem.at[part, unit]).wait()
    for distance in range(1, REACH + 1):
        @pl.when(layer_y + distance < SIDE)
        def _():
            @pl.loop(0, CHUNKS)
            def _(chunk):
                depth_copy(chunk, distance).wait_send()
    keep.wait()
    moved = attended.at[pl.ds(0, PEERS - 1)]
    pltpu.make_async_copy(moved, moved, out_send).wait()
    pltpu.make_async_copy(moved, moved, out_recv).wait()


def local(stream, depth_weights, depth_reach, norm_gain, qkv_weight):
    vmem = pl.BlockSpec(memory_space=pltpu.VMEM)
    smem = pl.BlockSpec(memory_space=pltpu.SMEM)
    hbm = pl.BlockSpec(memory_space=pl.ANY)
    layer, attended = pl.pallas_call(
        kernel,
        out_shape=(
            pltpu.VMEM((CHUNKS, ROWS, D), jnp.bfloat16),
            pltpu.VMEM((CHUNKS * ROWS, D), jnp.bfloat16),
        ),
        in_specs=[smem, smem, hbm, vmem, hbm],
        out_specs=(vmem,) * 2,
        scratch_shapes=[
            pltpu.VMEM((CHUNKS, ROWS, D), jnp.bfloat16),
            pltpu.VMEM((CHUNKS, PEERS, ROWS, D), jnp.bfloat16),
            pltpu.VMEM((REACH, CHUNKS, ROWS, D), jnp.bfloat16),
            pltpu.VMEM((D * 6, HD), jnp.bfloat16),
            pltpu.VMEM((W_ROWS * 6, HD), jnp.float32),
            pltpu.VMEM((D, 6 * HD), jnp.bfloat16),
            pltpu.VMEM((ROWS, D), jnp.float32),
            pltpu.VMEM((6, PEERS, CHUNKS, ROWS, HD), jnp.bfloat16),
            pltpu.VMEM((PEERS, HD, 2 * HD), jnp.bfloat16),
            pltpu.SemaphoreType.DMA((2, UNITS)),
            pltpu.SemaphoreType.DMA((2, UNITS, PEERS + 1)),
            pltpu.SemaphoreType.DMA((REACH, CHUNKS)),
            pltpu.SemaphoreType.DMA((REACH, CHUNKS)),
            pltpu.SemaphoreType.DMA,
            pltpu.SemaphoreType.DMA,
            pltpu.SemaphoreType.DMA,
            pltpu.SemaphoreType.DMA,
            pltpu.SemaphoreType.DMA,
            pltpu.SemaphoreType.REGULAR,
        ],
        compiler_params=pltpu.CompilerParams(
            collective_id=0, has_side_effects=True, vmem_limit_bytes=58 * 1024 * 1024
        ),
        cost_estimate=pl.CostEstimate(
            flops=16_000_000_000, bytes_accessed=12_000_000, transcendentals=5_000_000
        ),
    )(
        depth_weights, depth_reach,
        stream.reshape(CHUNKS, ROWS, D), norm_gain, jnp.transpose(qkv_weight[0], (0, 2, 1, 3)).reshape(D * 6, HD),
    )
    return layer.reshape(stream.shape), attended[None]


def solution(mesh):
    placed = (
        P("section", "seq", None),
        P("section", None),
        P("section"),
        P("section", None),
        P("section", None, "seq", None, None),
    )
    return jax.shard_map(
        local,
        mesh=mesh,
        in_specs=placed,
        out_specs=(P("section", "seq", None), P("section", "seq", None)),
        check_vma=False,
    )
```

```python
import jax
import jax.numpy as jnp
from jax import lax
from jax.experimental import pallas as pl
from jax.experimental.pallas import tpu as pltpu
from jax.sharding import PartitionSpec as P

MESH = pl.DeviceIdType.MESH
SIDE = 4
PEERS = SIDE * SIDE
CHUNKS = 8
ROWS = 16
SPACING = 4
REACH = 3
D = 4096
HD = 128
W_ROWS = 256
LAGS = (2, 4, 6, 8)
HEAD_START = 7
PARTS = 2
UNITS = CHUNKS * PARTS
WIDTH = D // PARTS
SPLIT = 1664


def wrap(value):
    return lax.rem(value + 2 * SIDE, SIDE)


def kernel(
    weights_ref, reach_ref, stream_hbm, gain_ref, w_hbm,
    layer_ref, out_ref,
    stream_ref, gathered, earlier, w_raw, w_wide, w_ref, mix, qkv, attended,
    send_sem, recv_sem, depth_send, depth_recv, w_sem, out_send, out_recv, own_sem, stream_sem, turn_sem,
):
    section = lax.axis_index("section")
    me = lax.axis_index("seq")
    layer_y = section // SPACING
    x, z = me // SIDE, lax.rem(me, SIDE)

    barrier = pltpu.get_barrier_semaphore()
    for step in range(1, PEERS):
        pl.semaphore_signal(
            barrier, inc=1,
            device_id={"seq": lax.rem(me + step, PEERS)}, device_id_type=MESH,
        )
    for step in range(1, SIDE):
        pl.semaphore_signal(
            barrier, inc=1,
            device_id={"section": lax.rem(section + step * SPACING, SIDE * SPACING)},
            device_id_type=MESH,
        )
    mate = section + 1 - 2 * lax.rem(section, 2)
    pl.semaphore_signal(barrier, inc=1, device_id={"section": mate}, device_id_type=MESH)
    stream_copy = pltpu.make_async_copy(stream_hbm, stream_ref, stream_sem)
    stream_copy.start()
    w_copy = pltpu.make_async_copy(w_hbm, w_raw, w_sem)
    w_copy.start()
    pl.semaphore_wait(barrier, PEERS - 1 + SIDE - 1 + 1)
    leads = lax.rem(section, 2) == 0

    def depth_copy(chunk, distance):
        return pltpu.make_async_remote_copy(
            src_ref=stream_ref.at[chunk],
            dst_ref=earlier.at[distance - 1, chunk],
            send_sem=depth_send.at[distance - 1, chunk],
            recv_sem=depth_recv.at[distance - 1, chunk],
            device_id={"section": lax.rem(section + distance * SPACING, SIDE * SPACING)},
            device_id_type=MESH,
        )

    def start_depth(chunk):
        for distance in range(1, REACH + 1):
            @pl.when(layer_y + distance < SIDE)
            def _():
                depth_copy(chunk, distance).start()

    def columns(part, unit, fold=None):
        begin = lax.rem(unit, PARTS) * WIDTH + (0 if part == 0 else SPLIT)
        size = SPLIT if part == 0 else WIDTH - SPLIT
        if fold is not None:
            near = size // 256 * 128
            begin, size = (begin, near) if fold == 0 else (begin + near, size - near)
        return pl.ds(pl.multiple_of(begin, 128), size)

    def place(part, major, minor):
        return minor * SIDE + major if part == 0 else major * SIDE + minor

    def block_copy(part, unit, origin, target, fold=None):
        block = gathered.at[unit // PARTS, origin, :, columns(part, unit, fold)]
        return pltpu.make_async_remote_copy(
            src_ref=block,
            dst_ref=block,
            send_sem=send_sem.at[part, unit],
            recv_sem=recv_sem.at[part, unit, PEERS if fold == 1 else origin],
            device_id={"seq": target},
            device_id_type=MESH,
        )

    def arrive(part, unit, origin, fold=None):
        block_copy(part, unit, origin, lax.rem(me + 1, PEERS), fold).wait_recv()

    spots = ((z, x), (x, z))

    def mix_rows(chunk):
        for distance in range(1, REACH + 1):
            @pl.when(layer_y >= distance)
            def _():
                depth_copy(chunk, distance).wait_recv()
        mix[...] = weights_ref[0, 0] * stream_ref[chunk].astype(jnp.float32)
        for distance in range(1, REACH + 1):
            @pl.when(layer_y >= distance)
            def _():
                now = jnp.where(distance <= reach_ref[0], weights_ref[0, distance], 0.0)
                mix[...] += now * earlier[distance - 1, chunk].astype(jnp.float32)
        value = mix[...]
        layer_ref[chunk] = value.astype(jnp.bfloat16)
        square = jnp.mean(value * value, axis=-1, keepdims=True)
        gathered[chunk, me] = (value * lax.rsqrt(square + 1e-05) * gain_ref[...]).astype(
            jnp.bfloat16
        )
    def own(unit):
        @pl.when(lax.rem(unit, PARTS) == 0)
        def _():
            mix_rows(unit // PARTS)

        for part in (0, 1):
            major, minor = spots[part]
            for by in (1, -1):
                block_copy(part, unit, me, place(part, wrap(major + by), minor)).start()
            for by in (1, -1):
                block_copy(part, unit, me, place(part, major, wrap(minor + by))).start()

    def aside(part, unit, origin):
        major, minor = spots[part]
        for side in (1, -1):
            block_copy(part, unit, origin, place(part, major, wrap(minor + side))).start()

    def spread_near(unit):
        for part in (0, 1):
            major, minor = spots[part]
            for fold, by in enumerate((-1, 1)):
                origin = place(part, wrap(major + by), minor)
                arrive(part, unit, origin)
                block_copy(part, unit, origin, place(part, wrap(major - by), minor), fold).start()
                aside(part, unit, origin)

    def spread_far(unit):
        for part in (0, 1):
            major, minor = spots[part]
            origin = place(part, wrap(major + 2), minor)
            for fold in (0, 1):
                arrive(part, unit, origin, fold)
            aside(part, unit, origin)

    rows_of = ((0, 1), (-1, -1), (1, -1), (2, 1))

    def relay(unit, rows):
        for by, way in rows:
            for part in (0, 1):
                major, minor = spots[part]
                origin = place(part, wrap(major + by), wrap(minor - way))
                arrive(part, unit, origin)
                block_copy(part, unit, origin, place(part, major, wrap(minor + way))).start()

    def finish(unit):
        for by, way in rows_of:
            for part in (0, 1):
                major, minor = spots[part]
                row = wrap(major + by)
                arrive(part, unit, place(part, row, wrap(minor + way)))
                arrive(part, unit, place(part, row, wrap(minor + 2)))

        @pl.when(lax.rem(unit, PARTS) == PARTS - 1)
        def _():
            project(unit // PARTS)

    def project(chunk):
        block = gathered[chunk].reshape(PEERS * ROWS, D)
        for tile in range(3):
            product = jnp.dot(
                block, w_ref[:, tile * 256:(tile + 1) * 256],
                preferred_element_type=jnp.float32,
            ).astype(jnp.bfloat16)
            for half in range(2):
                qkv[2 * tile + half, :, chunk] = product[
                    :, half * HD:(half + 1) * HD
                ].reshape(PEERS, ROWS, HD)

    stream_copy.wait()

    @pl.when(jnp.logical_not(leads))
    def _():
        pl.semaphore_wait(turn_sem, 1)

    start_depth(0)

    w_copy.wait()

    @pl.loop(0, D // W_ROWS)
    def _(part):
        begin = pl.multiple_of(part * W_ROWS, W_ROWS)
        w_wide[...] = w_raw[pl.ds(pl.multiple_of(part * W_ROWS * 6, W_ROWS * 6), W_ROWS * 6)].astype(
            jnp.float32
        )
        for piece in range(6):
            w_ref[pl.ds(begin, W_ROWS), piece * HD:(piece + 1) * HD] = w_wide[
                pl.ds(piece, W_ROWS, stride=6)
            ].astype(jnp.bfloat16)

    start_depth(1)

    @pl.loop(0, UNITS + LAGS[3])
    def _(step):
        def when(lag, work):
            @pl.when((step >= lag) & (step < UNITS + lag))
            def _():
                work(step - lag)

        when(0, own)

        @pl.when((lax.rem(step, PARTS) == 0) & (step // PARTS + 2 < CHUNKS))
        def _():
            start_depth(step // PARTS + 2)

        when(LAGS[0], spread_near)
        when(LAGS[1], lambda unit: relay(unit, rows_of[:3]))

        @pl.when(leads & (step == HEAD_START))
        def _():
            pl.semaphore_signal(turn_sem, inc=1, device_id={"section": mate}, device_id_type=MESH)

        when(LAGS[1], spread_far)
        when(LAGS[2], lambda unit: relay(unit, rows_of[3:]))
        when(LAGS[3], finish)

    scale = (HD ** -0.5) * 1.4426950408889634
    across = (((1,), (1,)), ((), ()))

    def attend(block):
        size = 2 * CHUNKS * ROWS
        row = lax.broadcasted_iota(jnp.int32, (size, size), 0)
        column = lax.broadcasted_iota(jnp.int32, (size, size), 1)
        for head in range(2):
            query = qkv[head, 2 * block:2 * block + 2].reshape(size, HD)
            pieces = [(2 * block, 2 * block + 2)]
            if block > 0:
                pieces.append((0, 2 * block))
            scores = []
            for begin, end in pieces:
                key = qkv[2 + head, begin:end].reshape((end - begin) * HD, HD)
                scores.append(
                    lax.dot_general(query, key, across, preferred_element_type=jnp.float32)
                )
            scores[0] = jnp.where(column <= row, scores[0], -jnp.inf)
            top = jnp.max(scores[0], axis=-1, keepdims=True)
            if block > 0:
                top = jnp.maximum(top, jnp.max(scores[1], axis=-1, keepdims=True))
            total, result = 0.0, 0.0
            for (begin, end), score in zip(pieces, scores):
                raw = jnp.exp2((score - top) * scale)
                total = total + jnp.sum(raw, axis=-1, keepdims=True)
                value = qkv[4 + head, begin:end].reshape((end - begin) * HD, HD)
                result = result + jnp.dot(
                    raw.astype(jnp.bfloat16), value, preferred_element_type=jnp.float32
                )
            attended[2 * block:2 * block + 2, :, head * HD:(head + 1) * HD] = (
                (result / total).astype(jnp.bfloat16).reshape(2, HD, HD)
            )

    lanes = out_ref.at[:, pl.ds(pl.multiple_of(me * 2 * HD, 2 * HD), 2 * HD)]
    keep = pltpu.make_async_copy(attended.at[me], lanes, own_sem)

    @pl.loop(0, PEERS // 2)
    def _(step):
        block = lax.rem(me // 2 + 1 + step, PEERS // 2)
        for variant in range(PEERS // 2):
            @pl.when(block == variant)
            def _():
                attend(variant)
        for half in range(2):
            target = 2 * block + half

            @pl.when(target != me)
            def _():
                pltpu.make_async_remote_copy(
                    src_ref=attended.at[target],
                    dst_ref=lanes,
                    send_sem=out_send,
                    recv_sem=out_recv,
                    device_id={"seq": target},
                    device_id_type=MESH,
                ).start()

    keep.start()
    for part in (0, 1):
        @pl.loop(0, UNITS)
        def _(unit):
            sent = gathered.at[unit // PARTS, pl.ds(0, PEERS - 1), :, columns(part, unit)]
            pltpu.make_async_copy(sent, sent, send_sem.at[part, unit]).wait()
    for distance in range(1, REACH + 1):
        @pl.when(layer_y + distance < SIDE)
        def _():
            @pl.loop(0, CHUNKS)
            def _(chunk):
                depth_copy(chunk, distance).wait_send()
    keep.wait()
    moved = attended.at[pl.ds(0, PEERS - 1)]
    pltpu.make_async_copy(moved, moved, out_send).wait()
    pltpu.make_async_copy(moved, moved, out_recv).wait()


def local(stream, depth_weights, depth_reach, norm_gain, qkv_weight):
    vmem = pl.BlockSpec(memory_space=pltpu.VMEM)
    smem = pl.BlockSpec(memory_space=pltpu.SMEM)
    hbm = pl.BlockSpec(memory_space=pl.ANY)
    layer, attended = pl.pallas_call(
        kernel,
        out_shape=(
            pltpu.VMEM((CHUNKS, ROWS, D), jnp.bfloat16),
            pltpu.VMEM((CHUNKS * ROWS, D), jnp.bfloat16),
        ),
        in_specs=[smem, smem, hbm, vmem, hbm],
        out_specs=(vmem,) * 2,
        scratch_shapes=[
            pltpu.VMEM((CHUNKS, ROWS, D), jnp.bfloat16),
            pltpu.VMEM((CHUNKS, PEERS, ROWS, D), jnp.bfloat16),
            pltpu.VMEM((REACH, CHUNKS, ROWS, D), jnp.bfloat16),
            pltpu.VMEM((D * 6, HD), jnp.bfloat16),
            pltpu.VMEM((W_ROWS * 6, HD), jnp.float32),
            pltpu.VMEM((D, 6 * HD), jnp.bfloat16),
            pltpu.VMEM((ROWS, D), jnp.float32),
            pltpu.VMEM((6, PEERS, CHUNKS, ROWS, HD), jnp.bfloat16),
            pltpu.VMEM((PEERS, HD, 2 * HD), jnp.bfloat16),
            pltpu.SemaphoreType.DMA((2, UNITS)),
            pltpu.SemaphoreType.DMA((2, UNITS, PEERS + 1)),
            pltpu.SemaphoreType.DMA((REACH, CHUNKS)),
            pltpu.SemaphoreType.DMA((REACH, CHUNKS)),
            pltpu.SemaphoreType.DMA,
            pltpu.SemaphoreType.DMA,
            pltpu.SemaphoreType.DMA,
            pltpu.SemaphoreType.DMA,
            pltpu.SemaphoreType.DMA,
            pltpu.SemaphoreType.REGULAR,
        ],
        compiler_params=pltpu.CompilerParams(
            collective_id=0, has_side_effects=True, vmem_limit_bytes=58 * 1024 * 1024
        ),
        cost_estimate=pl.CostEstimate(
            flops=16_000_000_000, bytes_accessed=12_000_000, transcendentals=5_000_000
        ),
    )(
        depth_weights, depth_reach,
        stream.reshape(CHUNKS, ROWS, D), norm_gain, jnp.transpose(qkv_weight[0], (0, 2, 1, 3)).reshape(D * 6, HD),
    )
    return layer.reshape(stream.shape), attended[None]


def solution(mesh):
    placed = (
        P("section", "seq", None),
        P("section", None),
        P("section"),
        P("section", None),
        P("section", None, "seq", None, None),
    )
    return jax.shard_map(
        local,
        mesh=mesh,
        in_specs=placed,
        out_specs=(P("section", "seq", None), P("section", "seq", None)),
        check_vma=False,
    )
```
